32 devices in a mesh: dp: 4 (over y, x), row: 2 (over core), col: 4 (over z).
Axes of the slice: x: 2, y: 2, z: 4, core: 2. Of those that a mesh axis runs over, the one named last changes fastest.
Arguments:
- pixels: bfloat16 [4, 64, 384, 256], P('dp', 'row', 'col'), may hold values from -6 to 6
- hidden_pre: bfloat16 [4, 32, 192, 256], P('dp', 'row', 'col'), may hold values from -6 to 6
- upstream: bfloat16 [4, 16, 96, 512], P('dp', 'row', 'col'), may hold values from -6 to 6
- kernel_first: bfloat16 [3, 3, 256, 256], replicated, may hold values from -0.125 to 0.125
- kernel_second: bfloat16 [3, 3, 256, 512], replicated, may hold values from -0.125 to 0.125
Outputs:
- grad_pixels: bfloat16 [4, 64, 384, 256], P('dp', 'row', 'col')
- grad_kernel_first: float32 [2304, 256], P(('row', 'col'))
- grad_kernel_second: float32 [2304, 512], P(('row', 'col'))
The draws below stay inside these ranges and needn't reach their ends.
All inputs are finite; a program needn't handle non-finite values.
Results may differ from the reference program's by a relative error of at most 0.0049.
Values may be sent and summed in bfloat16 or wider, within the bound.
A program may use at most 64 MiB of HBM per device.

```python
import math
import jax
import jax.numpy as jnp
from jax import lax

C0 = 256
C1 = 256
C2 = 512
SLIDES = 4
H2 = 16
W2 = 96
H1 = 32
W1 = 192
H0 = 64
W0 = 384


def block_scale(rng, shape, cuts, least, largest):
    loudness, own = 1.0, jax.random.fold_in(rng, 6)
    for axis_at, shards_of in cuts:
        draws = jnp.exp(jax.random.uniform(jax.random.fold_in(own, axis_at), (shards_of,), jnp.float32, least / len(cuts), largest / len(cuts)))
        loudness = loudness * jnp.repeat(draws, shape[axis_at] // shards_of).reshape([-1 if axis == axis_at else 1 for axis in range(len(shape))])
    return loudness


def noise(rng, shape, deviation, most, cuts=(), held_as=jnp.bfloat16):
    array = deviation * jax.random.normal(rng, shape, jnp.float32)
    if cuts:
        array = array * block_scale(rng, shape, cuts, -0.22, 0.18)
    return jnp.clip(array, -most, most).astype(held_as)


def setup_inputs(seed: int = 0) -> dict:
    splits = jax.random.split(jax.random.key(seed), 6)
    return {
        "pixels": noise(splits[0], (SLIDES, H0, W0, C0), 1.0, 6.0, ((0, 4), (1, 2), (2, 4))),
        "hidden_pre": noise(splits[1], (SLIDES, H1, W1, C1), 1.0, 6.0, ((0, 4), (1, 2), (2, 4))),
        "upstream": noise(splits[2], (SLIDES, H2, W2, C2), 1.0, 6.0, ((0, 4), (1, 2), (2, 4))),
        "kernel_first": noise(splits[3], (3, 3, C0, C1), (9 * C0) ** -0.5, 0.125),
        "kernel_second": noise(splits[4], (3, 3, C1, C2), (9 * C1) ** -0.5, 0.125),
    }


def convolve(field_in, kernel):
    return lax.conv_general_dilated(field_in, kernel, (2, 2), ((1, 1), (1, 1)), dimension_numbers=('NHWC', 'HWIO', 'NHWC'), precision=lax.Precision.HIGHEST)

def one_slide(slide_items, kernel_one, kernel_two):
    slide_pixels, slide_pre, slide_up = slide_items
    source = slide_pixels[None].astype(jnp.float32)
    hidden = slide_pre[None].astype(jnp.float32)
    active = jnp.maximum(hidden, 0.0)
    cotangent = slide_up[None].astype(jnp.float32)
    _, pull_second = jax.vjp(convolve, active, kernel_two)
    grad_active, grad_two = pull_second(cotangent)
    masked = jnp.where(hidden > 0.0, grad_active, 0.0).astype(jnp.bfloat16)
    masked = lax.optimization_barrier(masked).astype(jnp.float32)
    _, pull_first = jax.vjp(convolve, source, kernel_one)
    grad_source, grad_one = pull_first(masked)
    return (grad_source[0].astype(jnp.bfloat16), grad_one, grad_two)

def reference(pixels, hidden_pre, upstream, kernel_first, kernel_second):
    kernel_one = kernel_first.astype(jnp.float32)
    kernel_two = kernel_second.astype(jnp.float32)
    grad_pixels, grads_one, grads_two = lax.map(lambda slide_items: one_slide(slide_items, kernel_one, kernel_two), (pixels, hidden_pre, upstream))
    count_one = hidden_pre.shape[0] * hidden_pre.shape[1] * hidden_pre.shape[2]
    count_two = upstream.shape[0] * upstream.shape[1] * upstream.shape[2]
    grad_kernel_first = (lax.optimization_barrier(jnp.sum(grads_one, axis=0)) / math.sqrt(count_one)).reshape(9 * C0, C1)
    grad_kernel_second = (lax.optimization_barrier(jnp.sum(grads_two, axis=0)) / math.sqrt(count_two)).reshape(9 * C1, C2)
    return (grad_pixels, grad_kernel_first, grad_kernel_second)
```

```python
import functools
import math

import jax
import jax.numpy as jnp
from jax import lax
from jax.experimental import pallas as pl
from jax.experimental.pallas import tpu as pltpu
from jax.sharding import PartitionSpec as P

MESH = pl.DeviceIdType.MESH
F32 = jnp.float32
BF16 = jnp.bfloat16
NAMES = ("dp", "row", "col")


def peer(**changes):
    return tuple(changes.get(name, lax.axis_index(name)) for name in NAMES)


def halo_kernel(
    rows_n, cols_n, up_ref, hid_ref, u_row, u_col, u_cor, h_row, h_col, h_cor,
    su_row, su_col, su_cor, sh_row, sh_col, sh_cor, send_sem, recv_sem,
):
    row, col = lax.axis_index("row"), lax.axis_index("col")
    has_above, has_left = row > 0, col > 0
    has_below, has_right = row < rows_n - 1, col < cols_n - 1
    barrier = pltpu.get_barrier_semaphore()
    senders = (
        (has_below, dict(row=row + 1)),
        (has_right, dict(col=col + 1)),
        (has_below & has_right, dict(row=row + 1, col=col + 1)),
    )
    targets = (
        (has_above, dict(row=row - 1)),
        (has_left, dict(col=col - 1)),
        (has_above & has_left, dict(row=row - 1, col=col - 1)),
    )
    for holds, change in senders:
        @pl.when(holds)
        def _():
            pl.semaphore_signal(barrier, inc=1, device_id=peer(**change), device_id_type=MESH)

    su_row[...] = up_ref[0, 0].astype(F32)
    sh_row[...] = hid_ref[0, 0].astype(F32)
    for i in range(su_col.shape[0]):
        su_col[i : i + 1] = up_ref[0, i].astype(F32)[0:1]
    for i in range(sh_col.shape[0]):
        sh_col[i : i + 1] = hid_ref[0, i].astype(F32)[0:1]
    su_cor[...] = up_ref[0, 0].astype(F32)[0:8]
    sh_cor[...] = hid_ref[0, 0].astype(F32)[0:8]

    above, left = has_above.astype(jnp.int32), has_left.astype(jnp.int32)

    @pl.when(has_above | has_left)
    def _():
        pl.semaphore_wait(barrier, above + left + above * left)

    pairs = (
        ((su_row, u_row), (sh_row, h_row)),
        ((su_col, u_col), (sh_col, h_col)),
        ((su_cor, u_cor), (sh_cor, h_cor)),
    )

    def copies(way, change):
        return [
            pltpu.make_async_remote_copy(
                src_ref=src, dst_ref=dst, send_sem=send_sem.at[2 * way + k],
                recv_sem=recv_sem.at[2 * way + k], device_id=peer(**change), device_id_type=MESH,
            )
            for k, (src, dst) in enumerate(pairs[way])
        ]

    for way, (holds, change) in enumerate(targets):
        @pl.when(holds)
        def _():
            for copy in copies(way, change):
                copy.start()

    for way, (holds, change) in enumerate(senders):
        @pl.when(holds)
        def _():
            for copy in copies(way, change):
                copy.wait_recv()

        @pl.when(jnp.logical_not(holds))
        def _():
            for _, dst in pairs[way]:
                dst[...] = jnp.zeros(dst.shape, dst.dtype)

    for way, (holds, change) in enumerate(targets):
        @pl.when(holds)
        def _():
            for copy in copies(way, change):
                copy.wait_send()


def exchange_halo(upstream, hidden, mesh):
    _, ur, uc, uw = upstream.shape
    _, hr, hc, hw = hidden.shape
    shapes = [(uc, uw), (ur, uw), (8, uw), (hc, hw), (hr, hw), (8, hw)]
    return pl.pallas_call(
        functools.partial(halo_kernel, mesh.shape["row"], mesh.shape["col"]),
        out_shape=[jax.ShapeDtypeStruct(s, F32) for s in shapes],
        in_specs=[pl.BlockSpec(memory_space=pltpu.VMEM)] * 2,
        out_specs=[pl.BlockSpec(memory_space=pltpu.VMEM)] * 6,
        scratch_shapes=[pltpu.VMEM(s, F32) for s in shapes]
        + [pltpu.SemaphoreType.DMA((6,)), pltpu.SemaphoreType.DMA((6,))],
        compiler_params=pltpu.CompilerParams(
            collective_id=0, has_side_effects=True, vmem_limit_bytes=16 * 2**20
        ),
    )(upstream, hidden)


TAPS = {0: ((1, 0),), 1: ((2, 0), (0, 1))}
LANE = {(0, 1): 0, (0, 0): 1, (1, 0): 2, (1, 1): 3}


def terms_of(pr, pc):
    found = []
    for a, sr in TAPS[pr]:
        for b, sc in TAPS[pc]:
            found.append((LANE[(sr, sc)], a, b, (sr, sc)))
    return sorted(found)


PARITIES = ((0, 0), (0, 1), (1, 0), (1, 1))


def dot_t(x, w):
    return lax.dot_general(x, w, (((1,), (1,)), ((), ())), preferred_element_type=F32)


def dot_0(x, y):
    return lax.dot_general(x, y, (((0,), (0,)), ((), ())), preferred_element_type=F32)


def compute_kernel(
    scale_one, scale_two, pix_ref, hid_ref, up_ref, u_row, u_col, u_cor, h_row, h_col, h_cor,
    k1_ref, k2_ref, out_ref, g_ref, uext, gext, eext, ucat, ecat, aact, pix32,
):
    _, ur, uc, uw = up_ref.shape
    _, hr, hc, hw = hid_ref.shape
    pw = pix_ref.shape[-1]
    ucp = uext.shape[1] - 8
    uext[0:ur, 0:uc] = up_ref[0].astype(F32)
    uext[ur, 0:uc] = u_row[...]
    for i in range(ur):
        uext[i, uc : uc + 1] = u_col[i : i + 1]
    uext[ur, uc : uc + 1] = u_cor[0:1]

    for (sr, sc), lane in LANE.items():
        part = uext[sr : sr + ur, sc : sc + uc].reshape(ur * uc, uw).astype(BF16)
        ucat[:, lane * uw : (lane + 1) * uw] = part

    for pr, pc in PARITIES:
        kr = ur + 1 - pr
        total = None
        for _, a, b, (sr, sc) in terms_of(pr, pc):
            u = uext[sr : sr + kr, sc : sc + ucp].reshape(kr * ucp, uw).astype(BF16)
            term = dot_t(u, k2_ref[a, b])
            total = term if total is None else total + term
        total = total.reshape(kr, ucp, hw)
        for k in range(kr):
            for lo in range(0, hw, 128):
                gext[lo // 128, 2 * k + pr, pl.ds(pc, ucp, stride=2), :] = total[k, :, lo : lo + 128]

    for p in range(hr + 1):
        hid = hid_ref[0, p].astype(F32) if p < hr else h_row[...]
        edge = h_col[p : p + 1] if p < hr else h_cor[0:1]
        for lo in range(0, hw, 128):
            cut = slice(lo, lo + 128)
            eext[p, 0:hc, cut] = jnp.where(hid[:, cut] > 0, gext[lo // 128, p, 0:hc], 0.0)
            eext[p, hc : hc + 1, cut] = jnp.where(
                edge[:, cut] > 0, gext[lo // 128, p, hc : hc + 1], 0.0
            )
            if p < hr:
                aact[lo // 128, p] = jnp.maximum(hid[:, cut], 0.0)

    for (sr, sc), lane in LANE.items():
        part = eext[sr : sr + hr, sc : sc + hc].reshape(hr * hc, hw).astype(BF16)
        ecat[:, lane * hw : (lane + 1) * hw] = part

    def put(tap, lanes, value):
        g_ref[pl.ds(tap * hw, hw), lanes] = value.astype(BF16)

    for pr, pc in PARITIES:
        parts = [
            jnp.stack([aact[h, 2 * k + pr, pl.ds(pc, uc, stride=2), :] for k in range(ur)])
            for h in range(hw // 128)
        ]
        act = jnp.concatenate(parts, axis=-1).reshape(ur * uc, hw).astype(BF16)
        terms = terms_of(pr, pc)
        first = terms[0][0]
        total = dot_0(act, ucat[:, first * uw : (first + len(terms)) * uw]) * scale_two
        for n, (_, a, b, _) in enumerate(terms):
            put(3 * a + b, pl.ds(hw, uw), total[:, n * uw : (n + 1) * uw])

    for h in range(pw // 128):
        pix32[h] = pix_ref[0, :, :, h * 128 : (h + 1) * 128].astype(F32)
    for pr, pc in PARITIES:
        parts = [
            jnp.stack([pix32[h, 2 * k + pr, pl.ds(pc, hc, stride=2), :] for k in range(hr)])
            for h in range(pw // 128)
        ]
        pix = jnp.concatenate(parts, axis=-1).reshape(hr * hc, pw).astype(BF16)
        terms = terms_of(pr, pc)
        first = terms[0][0]
        total = dot_0(pix, ecat[:, first * hw : (first + len(terms)) * hw]) * scale_one
        for n, (_, a, b, _) in enumerate(terms):
            put(3 * a + b, pl.ds(0, hw), total[:, n * hw : (n + 1) * hw])

    for pr, pc in PARITIES:
        total = None
        for lane, a, b, _ in terms_of(pr, pc):
            term = dot_t(ecat[:, lane * hw : (lane + 1) * hw], k1_ref[a, b])
            total = term if total is None else total + term
        total = total.reshape(hr, hc, pw)
        for k in range(hr):
            for h in range(pw // 128):
                pix32[h, 2 * k + pr, pl.ds(pc, hc, stride=2), :] = total[k, :, h * 128 : (h + 1) * 128]
    for h in range(pw // 128):
        out_ref[0, :, :, h * 128 : (h + 1) * 128] = pix32[h].astype(BF16)


def compute(pixels, hidden, upstream, halo, kernel_first, kernel_second, devices):
    _, ur, uc, uw = upstream.shape
    _, hr, hc, hw = hidden.shape
    _, pr, pc, pw = pixels.shape
    scale_one = 1.0 / math.sqrt(devices * hr * hc)
    scale_two = 1.0 / math.sqrt(devices * ur * uc)
    ucp = (uc // 8 + 1) * 8
    vmem = pl.BlockSpec(memory_space=pltpu.VMEM)
    return pl.pallas_call(
        functools.partial(compute_kernel, scale_one, scale_two),
        out_shape=[
            jax.ShapeDtypeStruct(pixels.shape, BF16),
            jax.ShapeDtypeStruct((9 * hw, hw + uw), BF16),
        ],
        in_specs=[vmem] * 11,
        out_specs=[vmem] * 2,
        scratch_shapes=[
            pltpu.VMEM((ur + 2, ucp + 8, uw), F32),
            pltpu.VMEM((hw // 128, hr + 2, 2 * ucp, 128), F32),
            pltpu.VMEM((hr + 1, hc + 8, hw), F32),
            pltpu.VMEM((ur * uc, 4 * uw), BF16),
            pltpu.VMEM((hr * hc, 4 * hw), BF16),
            pltpu.VMEM((hw // 128, hr, hc, 128), F32),
            pltpu.VMEM((pw // 128, pr, pc, 128), F32),
        ],
        compiler_params=pltpu.CompilerParams(vmem_limit_bytes=52 * 2**20),
    )(pixels, hidden, upstream, *halo, kernel_first, kernel_second)


def reduce_kernel(
    dps, rows_n, cols_n, g_ref, out_ref, acc1, in1, acc2, in2, in3, mine, in4,
    s1, r1, s2, r2, s3, r3, s4, r4,
):
    dp, row, col = (lax.axis_index(name) for name in NAMES)
    size, width = g_ref.shape[2:]
    half, lanes = size // 2, width // 2
    barrier = pltpu.get_barrier_semaphore()
    partners = (
        [dict(row=lax.rem(row + k, rows_n)) for k in range(1, rows_n)]
        + [dict(dp=lax.rem(dp + k, dps)) for k in range(1, dps)]
        + [dict(col=lax.rem(col + k, cols_n)) for k in range(1, cols_n)]
    )
    for change in partners:
        pl.semaphore_signal(barrier, inc=1, device_id=peer(**change), device_id_type=MESH)
    pl.semaphore_wait(barrier, len(partners))

    def remote(src, dst, send, recv, change):
        return pltpu.make_async_remote_copy(
            src_ref=src, dst_ref=dst, send_sem=send, recv_sem=recv,
            device_id=peer(**change), device_id_type=MESH,
        )

    def piece(ref, d):
        return ref.at[d // 2, d % 2]

    def target(me, k, n):
        return lax.rem(me + k, n)

    copies1, copies2, copies3, copies4 = {}, {}, {}, {}
    order = [lax.rem(col + j, cols_n) for j in range(1, cols_n)] + [col]
    for j, c in enumerate(order):
        for k in range(1, rows_n):
            to = target(row, k, rows_n)
            copy = remote(
                g_ref.at[to, c], in1.at[k - 1, j], s1.at[k - 1, j], r1.at[k - 1, j], dict(row=to)
            )
            copy.start()
            copies1[k, j] = copy
    for j, c in enumerate(order):
        for k in range(1, rows_n):
            copies1[k, j].wait_recv()
        total = g_ref[row, c].astype(F32)
        for k in range(1, rows_n):
            total = total + in1[k - 1, j].astype(F32)
        for y in range(2):
            for x in range(2):
                acc1[j, y, x] = total[y * half : (y + 1) * half, x * lanes : (x + 1) * lanes].astype(BF16)
        for k in range(1, dps):
            to = target(dp, k, dps)
            copy = remote(
                acc1.at[j, to // 2, to % 2], in2.at[k - 1, j], s2.at[k - 1, j], r2.at[k - 1, j],
                dict(dp=to),
            )
            copy.start()
            copies2[k, j] = copy
    for j, c in enumerate(order):
        for k in range(1, dps):
            copies2[k, j].wait_recv()
        total = acc1[j, dp // 2, dp % 2].astype(F32)
        for k in range(1, dps):
            total = total + in2[k - 1, j].astype(F32)
        acc2[j] = total.astype(BF16)
        if j < cols_n - 1:
            copy = remote(acc2.at[j], in3.at[j], s3.at[j], r3.at[j], dict(col=c))
            copy.start()
            copies3[j] = copy
    total = acc2[cols_n - 1].astype(F32)
    for j in range(cols_n - 1):
        copies3[j].wait_recv()
        total = total + in3[j].astype(F32)
    mine[...] = total.astype(BF16)
    for k in range(1, dps):
        to = target(dp, k, dps)
        copy = remote(mine, in4.at[dp // 2, dp % 2], s4.at[k - 1], r4.at[k - 1], dict(dp=to))
        copy.start()
        copies4[k] = copy
    in4[dp // 2, dp % 2] = mine[...]
    for k in range(1, dps):
        copies4[k].wait_recv()
    for y in range(2):
        for x in range(2):
            out_ref[y * half : (y + 1) * half, x * lanes : (x + 1) * lanes] = in4[y, x].astype(F32)
    for group in (copies1, copies2, copies3, copies4):
        for copy in group.values():
            copy.wait_send()


def reduce_gradients(g, mesh, shares):
    dps, rows_n, cols_n = (mesh.shape[name] for name in NAMES)
    size = g.shape[0] // shares
    padded = -(-size // 32) * 32
    width = g.shape[1]
    g = g.reshape(shares, size, width)
    if padded != size:
        g = jnp.pad(g, ((0, 0), (0, padded - size), (0, 0)))
    g = g.reshape(rows_n, cols_n, padded, width)
    half, lanes = padded // 2, width // 2
    dma = pltpu.SemaphoreType.DMA
    out = pl.pallas_call(
        functools.partial(reduce_kernel, dps, rows_n, cols_n),
        out_shape=jax.ShapeDtypeStruct((padded, width), F32),
        in_specs=[pl.BlockSpec(memory_space=pltpu.VMEM)],
        out_specs=pl.BlockSpec(memory_space=pltpu.VMEM),
        scratch_shapes=[
            pltpu.VMEM((cols_n, 2, 2, half, lanes), BF16),
            pltpu.VMEM((rows_n - 1, cols_n, padded, width), BF16),
            pltpu.VMEM((cols_n, half, lanes), BF16),
            pltpu.VMEM((dps - 1, cols_n, half, lanes), BF16),
            pltpu.VMEM((cols_n - 1, half, lanes), BF16),
            pltpu.VMEM((half, lanes), BF16),
            pltpu.VMEM((2, 2, half, lanes), BF16),
            dma((rows_n - 1, cols_n)), dma((rows_n - 1, cols_n)),
            dma((dps - 1, cols_n)), dma((dps - 1, cols_n)),
            dma((cols_n - 1,)), dma((cols_n - 1,)),
            dma((dps - 1,)), dma((dps - 1,)),
        ],
        compiler_params=pltpu.CompilerParams(
            collective_id=1, has_side_effects=True, vmem_limit_bytes=48 * 2**20
        ),
    )(g)
    return out[:size]


def solution(mesh):
    def per_device(pixels, hidden, upstream, kernel_first, kernel_second):
        devices = mesh.size
        shares = mesh.shape["row"] * mesh.shape["col"]
        halo = exchange_halo(upstream, hidden, mesh)
        grad_pixels, gradients = compute(
            pixels, hidden, upstream, halo, kernel_first, kernel_second, devices
        )
        total = reduce_gradients(gradients, mesh, shares)
        width = kernel_first.shape[-1]
        return grad_pixels, total[:, :width], total[:, width:]

    in_specs = (P("dp", "row", "col", None),) * 3 + (P(), P())
    out_specs = (P("dp", "row", "col", None), P(("row", "col"), None), P(("row", "col"), None))
    return jax.shard_map(
        per_device, mesh=mesh, in_specs=in_specs, out_specs=out_specs, check_vma=False
    )
```

```python
import functools
import math

import jax
import jax.numpy as jnp
from jax import lax
from jax.experimental import pallas as pl
from jax.experimental.pallas import tpu as pltpu
from jax.sharding import PartitionSpec as P

MESH = pl.DeviceIdType.MESH
F32 = jnp.float32
BF16 = jnp.bfloat16
NAMES = ("dp", "row", "col")


def peer(**changes):
    return tuple(changes.get(name, lax.axis_index(name)) for name in NAMES)


def halo_kernel(
    rows_n, cols_n, up_ref, hid_ref, u_row, u_col, u_cor, h_row, h_col, h_cor,
    su_row, su_col, su_cor, sh_row, sh_col, sh_cor, send_sem, recv_sem,
):
    row, col = lax.axis_index("row"), lax.axis_index("col")
    has_above, has_left = row > 0, col > 0
    has_below, has_right = row < rows_n - 1, col < cols_n - 1
    barrier = pltpu.get_barrier_semaphore()
    senders = (
        (has_below, dict(row=row + 1)),
        (has_right, dict(col=col + 1)),
        (has_below & has_right, dict(row=row + 1, col=col + 1)),
    )
    targets = (
        (has_above, dict(row=row - 1)),
        (has_left, dict(col=col - 1)),
        (has_above & has_left, dict(row=row - 1, col=col - 1)),
    )
    for holds, change in senders:
        @pl.when(holds)
        def _():
            pl.semaphore_signal(barrier, inc=1, device_id=peer(**change), device_id_type=MESH)

    su_row[...] = up_ref[0, 0].astype(F32)
    sh_row[...] = hid_ref[0, 0].astype(F32)
    for i in range(su_col.shape[0]):
        su_col[i : i + 1] = up_ref[0, i].astype(F32)[0:1]
    for i in range(sh_col.shape[0]):
        sh_col[i : i + 1] = hid_ref[0, i].astype(F32)[0:1]
    su_cor[...] = up_ref[0, 0].astype(F32)[0:8]
    sh_cor[...] = hid_ref[0, 0].astype(F32)[0:8]

    above, left = has_above.astype(jnp.int32), has_left.astype(jnp.int32)

    @pl.when(has_above | has_left)
    def _():
        pl.semaphore_wait(barrier, above + left + above * left)

    pairs = (
        ((su_row, u_row), (sh_row, h_row)),
        ((su_col, u_col), (sh_col, h_col)),
        ((su_cor, u_cor), (sh_cor, h_cor)),
    )

    def copies(way, change):
        return [
            pltpu.make_async_remote_copy(
                src_ref=src, dst_ref=dst, send_sem=send_sem.at[2 * way + k],
                recv_sem=recv_sem.at[2 * way + k], device_id=peer(**change), device_id_type=MESH,
            )
            for k, (src, dst) in enumerate(pairs[way])
        ]

    for way, (holds, change) in enumerate(targets):
        @pl.when(holds)
        def _():
            for copy in copies(way, change):
                copy.start()

    for way, (holds, change) in enumerate(senders):
        @pl.when(holds)
        def _():
            for copy in copies(way, change):
                copy.wait_recv()

        @pl.when(jnp.logical_not(holds))
        def _():
            for _, dst in pairs[way]:
                dst[...] = jnp.zeros(dst.shape, dst.dtype)

    for way, (holds, change) in enumerate(targets):
        @pl.when(holds)
        def _():
            for copy in copies(way, change):
                copy.wait_send()


def exchange_halo(upstream, hidden, mesh):
    _, ur, uc, uw = upstream.shape
    _, hr, hc, hw = hidden.shape
    shapes = [(uc, uw), (ur, uw), (8, uw), (hc, hw), (hr, hw), (8, hw)]
    return pl.pallas_call(
        functools.partial(halo_kernel, mesh.shape["row"], mesh.shape["col"]),
        out_shape=[jax.ShapeDtypeStruct(s, F32) for s in shapes],
        in_specs=[pl.BlockSpec(memory_space=pltpu.VMEM)] * 2,
        out_specs=[pl.BlockSpec(memory_space=pltpu.VMEM)] * 6,
        scratch_shapes=[pltpu.VMEM(s, F32) for s in shapes]
        + [pltpu.SemaphoreType.DMA((6,)), pltpu.SemaphoreType.DMA((6,))],
        compiler_params=pltpu.CompilerParams(
            collective_id=0, has_side_effects=True, vmem_limit_bytes=16 * 2**20
        ),
    )(upstream, hidden)


TAPS = {0: ((1, 0),), 1: ((2, 0), (0, 1))}
LANE = {(0, 1): 0, (0, 0): 1, (1, 0): 2, (1, 1): 3}


def terms_of(pr, pc):
    found = []
    for a, sr in TAPS[pr]:
        for b, sc in TAPS[pc]:
            found.append((LANE[(sr, sc)], a, b, (sr, sc)))
    return sorted(found)


PARITIES = ((0, 0), (0, 1), (1, 0), (1, 1))


def dot_t(x, w):
    return lax.dot_general(x, w, (((1,), (1,)), ((), ())), preferred_element_type=F32)


def dot_0(x, y):
    return lax.dot_general(x, y, (((0,), (0,)), ((), ())), preferred_element_type=F32)


def compute_kernel(
    scale_one, scale_two, pix_ref, hid_ref, up_ref, u_row, u_col, u_cor, h_row, h_col, h_cor,
    k1_ref, k2_ref, out_ref, g_ref, uext, gext, eext, ucat, ecat, aact, pix32,
):
    _, ur, uc, uw = up_ref.shape
    _, hr, hc, hw = hid_ref.shape
    pw = pix_ref.shape[-1]
    ucp = uext.shape[1] - 8
    uext[0:ur, 0:uc] = up_ref[0].astype(F32)
    uext[ur, 0:uc] = u_row[...]
    for i in range(ur):
        uext[i, uc : uc + 1] = u_col[i : i + 1]
    uext[ur, uc : uc + 1] = u_cor[0:1]

    for (sr, sc), lane in LANE.items():
        part = uext[sr : sr + ur, sc : sc + uc].reshape(ur * uc, uw).astype(BF16)
        ucat[:, lane * uw : (lane + 1) * uw] = part

    for pr, pc in PARITIES:
        kr = ur + 1 - pr
        total = None
        for _, a, b, (sr, sc) in terms_of(pr, pc):
            u = uext[sr : sr + kr, sc : sc + ucp].reshape(kr * ucp, uw).astype(BF16)
            term = dot_t(u, k2_ref[a, b])
            total = term if total is None else total + term
        total = total.reshape(kr, ucp, hw)
        for k in range(kr):
            for lo in range(0, hw, 128):
                gext[lo // 128, 2 * k + pr, pl.ds(pc, ucp, stride=2), :] = total[k, :, lo : lo + 128]

    for p in range(hr + 1):
        hid = hid_ref[0, p].astype(F32) if p < hr else h_row[...]
        edge = h_col[p : p + 1] if p < hr else h_cor[0:1]
        for lo in range(0, hw, 128):
            cut = slice(lo, lo + 128)
            eext[p, 0:hc, cut] = jnp.where(hid[:, cut] > 0, gext[lo // 128, p, 0:hc], 0.0)
            eext[p, hc : hc + 1, cut] = jnp.where(
                edge[:, cut] > 0, gext[lo // 128, p, hc : hc + 1], 0.0
            )
            if p < hr:
                aact[lo // 128, p] = jnp.maximum(hid[:, cut], 0.0)

    for (sr, sc), lane in LANE.items():
        part = eext[sr : sr + hr, sc : sc + hc].reshape(hr * hc, hw).astype(BF16)
        ecat[:, lane * hw : (lane + 1) * hw] = part

    def put(tap, lanes, value):
        g_ref[pl.ds(tap * hw, hw), lanes] = value.astype(BF16)

    for pr, pc in PARITIES:
        parts = [
            jnp.stack([aact[h, 2 * k + pr, pl.ds(pc, uc, stride=2), :] for k in range(ur)])
            for h in range(hw // 128)
        ]
        act = jnp.concatenate(parts, axis=-1).reshape(ur * uc, hw).astype(BF16)
        terms = terms_of(pr, pc)
        first = terms[0][0]
        total = dot_0(act, ucat[:, first * uw : (first + len(terms)) * uw]) * scale_two
        for n, (_, a, b, _) in enumerate(terms):
            put(3 * a + b, pl.ds(hw, uw), total[:, n * uw : (n + 1) * uw])

    for h in range(pw // 128):
        pix32[h] = pix_ref[0, :, :, h * 128 : (h + 1) * 128].astype(F32)
    for pr, pc in PARITIES:
        parts = [
            jnp.stack([pix32[h, 2 * k + pr, pl.ds(pc, hc, stride=2), :] for k in range(hr)])
            for h in range(pw // 128)
        ]
        pix = jnp.concatenate(parts, axis=-1).reshape(hr * hc, pw).astype(BF16)
        terms = terms_of(pr, pc)
        first = terms[0][0]
        total = dot_0(pix, ecat[:, first * hw : (first + len(terms)) * hw]) * scale_one
        for n, (_, a, b, _) in enumerate(terms):
            put(3 * a + b, pl.ds(0, hw), total[:, n * hw : (n + 1) * hw])

    for pr, pc in PARITIES:
        total = None
        for lane, a, b, _ in terms_of(pr, pc):
            term = dot_t(ecat[:, lane * hw : (lane + 1) * hw], k1_ref[a, b])
            total = term if total is None else total + term
        total = total.reshape(hr, hc, pw)
        for k in range(hr):
            for h in range(pw // 128):
                pix32[h, 2 * k + pr, pl.ds(pc, hc, stride=2), :] = total[k, :, h * 128 : (h + 1) * 128]
    for h in range(pw // 128):
        out_ref[0, :, :, h * 128 : (h + 1) * 128] = pix32[h].astype(BF16)


def compute(pixels, hidden, upstream, halo, kernel_first, kernel_second, devices):
    _, ur, uc, uw = upstream.shape
    _, hr, hc, hw = hidden.shape
    _, pr, pc, pw = pixels.shape
    scale_one = 1.0 / math.sqrt(devices * hr * hc)
    scale_two = 1.0 / math.sqrt(devices * ur * uc)
    ucp = (uc // 8 + 1) * 8
    vmem = pl.BlockSpec(memory_space=pltpu.VMEM)
    return pl.pallas_call(
        functools.partial(compute_kernel, scale_one, scale_two),
        out_shape=[
            jax.ShapeDtypeStruct(pixels.shape, BF16),
            jax.ShapeDtypeStruct((9 * hw, hw + uw), BF16),
        ],
        in_specs=[vmem] * 11,
        out_specs=[vmem] * 2,
        scratch_shapes=[
            pltpu.VMEM((ur + 2, ucp + 8, uw), F32),
            pltpu.VMEM((hw // 128, hr + 2, 2 * ucp, 128), F32),
            pltpu.VMEM((hr + 1, hc + 8, hw), F32),
            pltpu.VMEM((ur * uc, 4 * uw), BF16),
            pltpu.VMEM((hr * hc, 4 * hw), BF16),
            pltpu.VMEM((hw // 128, hr, hc, 128), F32),
            pltpu.VMEM((pw // 128, pr, pc, 128), F32),
        ],
        compiler_params=pltpu.CompilerParams(vmem_limit_bytes=52 * 2**20),
    )(pixels, hidden, upstream, *halo, kernel_first, kernel_second)


def reduce_kernel(
    dps, rows_n, cols_n, g_ref, out_ref, acc1, in1, acc_a, in_a, acc_b, in_b, in3, mine, in4,
    s1, r1, sa, ra, sb, rb, s3, r3, s4, r4,
):
    dp, row, col = (lax.axis_index(name) for name in NAMES)
    size, width = g_ref.shape[2:]
    half, lanes = size // 2, width // 2
    bits = (dp // 2, dp % 2)
    across = (dict(dp=lax.rem(dp + 2, 4)), dict(dp=dp + 1 - 2 * (dp % 2)))
    barrier = pltpu.get_barrier_semaphore()
    partners = (
        [dict(row=lax.rem(row + k, rows_n)) for k in range(1, rows_n)]
        + [dict(dp=lax.rem(dp + k, dps)) for k in range(1, dps)]
        + [dict(col=lax.rem(col + k, cols_n)) for k in range(1, cols_n)]
    )
    for change in partners:
        pl.semaphore_signal(barrier, inc=1, device_id=peer(**change), device_id_type=MESH)
    pl.semaphore_wait(barrier, len(partners))
    started = []

    def send(src, dst, send_sem, recv_sem, change):
        copy = pltpu.make_async_remote_copy(
            src_ref=src, dst_ref=dst, send_sem=send_sem, recv_sem=recv_sem,
            device_id=peer(**change), device_id_type=MESH,
        )
        copy.start()
        started.append(copy)
        return copy

    copies1, copies_a, copies_b, copies3, copies4 = {}, {}, {}, {}, {}
    order = [lax.rem(col + j, cols_n) for j in range(1, cols_n)] + [col]
    for j, c in enumerate(order):
        for k in range(1, rows_n):
            to = lax.rem(row + k, rows_n)
            copies1[k, j] = send(
                g_ref.at[to, c], in1.at[k - 1, j], s1.at[k - 1, j], r1.at[k - 1, j], dict(row=to)
            )

    def first_stage(j):
        for k in range(1, rows_n):
            copies1[k, j].wait_recv()
        for y in range(2):
            for x in range(2):
                rows, cut = pl.ds(y * half, half), pl.ds(x * lanes, lanes)
                total = g_ref[row, order[j], rows, cut].astype(F32)
                for k in range(1, rows_n):
                    total = total + in1[k - 1, j, rows, cut].astype(F32)
                at = (y, x) if j % 2 == 0 else (x, y)
                acc1[j, at[0], at[1]] = total.astype(BF16)
        way = j % 2
        copies_a[j] = send(
            acc1.at[j, 1 - bits[way]], in_a.at[j], sa.at[j], ra.at[j], across[way]
        )

    def second_stage(j):
        way = j % 2
        copies_a[j].wait_recv()
        there = 1 - bits[1 - way]
        acc_a[j] = (
            acc1[j, bits[way], there].astype(F32) + in_a[j, there].astype(F32)
        ).astype(BF16)
        copies_b[j] = send(acc_a.at[j], in_b.at[j], sb.at[j], rb.at[j], across[1 - way])

    def third_stage(j):
        way = j % 2
        here = bits[1 - way]
        total = acc1[j, bits[way], here].astype(F32) + in_a[j, here].astype(F32)
        copies_b[j].wait_recv()
        total = total + in_b[j].astype(F32)
        if j == cols_n - 1:
            return total
        acc_b[j] = total.astype(BF16)
        copies3[j] = send(acc_b.at[j], in3.at[j], s3.at[j], r3.at[j], dict(col=order[j]))

    total = None
    for step in range(cols_n + 3):
        if step < cols_n:
            first_stage(step)
        if 0 <= step - 2 < cols_n:
            second_stage(step - 2)
        if 0 <= step - 3 < cols_n:
            total = third_stage(step - 3)
    for j in range(cols_n - 1):
        copies3[j].wait_recv()
        total = total + in3[j].astype(F32)
    mine[...] = total.astype(BF16)
    for k in range(1, dps):
        to = lax.rem(dp + k, dps)
        copies4[k] = send(
            mine, in4.at[bits[0], bits[1]], s4.at[k - 1], r4.at[k - 1], dict(dp=to)
        )
    in4[bits[0], bits[1]] = mine[...]
    for k in range(1, dps):
        copies4[k].wait_recv()
    for y in range(2):
        for x in range(2):
            out_ref[y * half : (y + 1) * half, x * lanes : (x + 1) * lanes] = in4[y, x].astype(F32)
    for copy in started:
        copy.wait_send()


def reduce_gradients(g, mesh, shares):
    dps, rows_n, cols_n = (mesh.shape[name] for name in NAMES)
    size = g.shape[0] // shares
    padded = -(-size // 32) * 32
    width = g.shape[1]
    g = g.reshape(shares, size, width)
    if padded != size:
        g = jnp.pad(g, ((0, 0), (0, padded - size), (0, 0)))
    g = g.reshape(rows_n, cols_n, padded, width)
    half, lanes = padded // 2, width // 2
    dma = pltpu.SemaphoreType.DMA
    out = pl.pallas_call(
        functools.partial(reduce_kernel, dps, rows_n, cols_n),
        out_shape=jax.ShapeDtypeStruct((padded, width), F32),
        in_specs=[pl.BlockSpec(memory_space=pltpu.VMEM)],
        out_specs=pl.BlockSpec(memory_space=pltpu.VMEM),
        scratch_shapes=[
            pltpu.VMEM((cols_n, 2, 2, half, lanes), BF16),
            pltpu.VMEM((rows_n - 1, cols_n, padded, width), BF16),
            pltpu.VMEM((cols_n, half, lanes), BF16),
            pltpu.VMEM((cols_n, 2, half, lanes), BF16),
            pltpu.VMEM((cols_n - 1, half, lanes), BF16),
            pltpu.VMEM((cols_n, half, lanes), BF16),
            pltpu.VMEM((cols_n - 1, half, lanes), BF16),
            pltpu.VMEM((half, lanes), BF16),
            pltpu.VMEM((2, 2, half, lanes), BF16),
            dma((rows_n - 1, cols_n)), dma((rows_n - 1, cols_n)),
            dma((cols_n,)), dma((cols_n,)), dma((cols_n,)), dma((cols_n,)),
            dma((cols_n - 1,)), dma((cols_n - 1,)),
            dma((dps - 1,)), dma((dps - 1,)),
        ],
        compiler_params=pltpu.CompilerParams(
            collective_id=1, has_side_effects=True, vmem_limit_bytes=48 * 2**20
        ),
    )(g)
    return out[:size]


def solution(mesh):
    def per_device(pixels, hidden, upstream, kernel_first, kernel_second):
        devices = mesh.size
        shares = mesh.shape["row"] * mesh.shape["col"]
        halo = exchange_halo(upstream, hidden, mesh)
        grad_pixels, gradients = compute(
            pixels, hidden, upstream, halo, kernel_first, kernel_second, devices
        )
        total = reduce_gradients(gradients, mesh, shares)
        width = kernel_first.shape[-1]
        return grad_pixels, total[:, :width], total[:, width:]

    in_specs = (P("dp", "row", "col", None),) * 3 + (P(), P())
    out_specs = (P("dp", "row", "col", None), P(("row", "col"), None), P(("row", "col"), None))
    return jax.shard_map(
        per_device, mesh=mesh, in_specs=in_specs, out_specs=out_specs, check_vma=False
    )
```

```python
import functools
import math

import jax
import jax.numpy as jnp
from jax import lax
from jax.experimental import pallas as pl
from jax.experimental.pallas import tpu as pltpu
from jax.sharding import PartitionSpec as P

MESH = pl.DeviceIdType.MESH
F32 = jnp.float32
BF16 = jnp.bfloat16
NAMES = ("dp", "row", "col")


def peer(**changes):
    return tuple(changes.get(name, lax.axis_index(name)) for name in NAMES)


TAPS = {0: ((1, 0),), 1: ((2, 0), (0, 1))}
LANE = {(0, 1): 0, (0, 0): 1, (1, 0): 2, (1, 1): 3}


def terms_of(pr, pc):
    found = []
    for a, sr in TAPS[pr]:
        for b, sc in TAPS[pc]:
            found.append((LANE[(sr, sc)], a, b, (sr, sc)))
    return sorted(found)


PARITIES = ((0, 0), (0, 1), (1, 0), (1, 1))


def dot_t(x, w):
    return lax.dot_general(x, w, (((1,), (1,)), ((), ())), preferred_element_type=F32)


def dot_0(x, y):
    return lax.dot_general(x, y, (((0,), (0,)), ((), ())), preferred_element_type=F32)


def fused_kernel(
    dps, rows_n, cols_n, share, padded, scale_one, scale_two,
    pix_hbm, hid_hbm, up_hbm, k1_hbm, k2_hbm, out_hbm, g1_out, g2_out,
    pix_ref, hid_ref, up_ref, k1_ref, k2_ref, out_ref,
    u_row, u_col, u_cor, h_row, h_col, h_cor,
    su_row, su_col, su_cor, sh_row, sh_col, sh_cor,
    uext, gext, eext, ucat, ecat, aact, pix32, g_ref,
    acc1, in1, acc2, in2, in3, mine, in4,
    local_sem, halo_send, halo_recv, s1, r1, s2, r2, s3, r3, s4, r4,
):
    dp, row, col = (lax.axis_index(name) for name in NAMES)
    _, ur, uc, uw = up_ref.shape
    _, hr, hc, hw = hid_ref.shape
    pw = pix_ref.shape[-1]
    ucp = uext.shape[1] - 8
    width = hw + uw
    half, lanes = padded // 2, width // 2
    local = [
        pltpu.make_async_copy(src, dst, local_sem.at[n])
        for n, (src, dst) in enumerate(
            ((up_hbm, up_ref), (hid_hbm, hid_ref), (pix_hbm, pix_ref), (k2_hbm, k2_ref), (k1_hbm, k1_ref))
        )
    ]
    for copy in local:
        copy.start()

    has_above, has_left = row > 0, col > 0
    has_below, has_right = row < rows_n - 1, col < cols_n - 1
    senders = (
        (has_below, dict(row=row + 1)),
        (has_right, dict(col=col + 1)),
        (has_below & has_right, dict(row=row + 1, col=col + 1)),
    )
    targets = (
        (has_above, dict(row=row - 1)),
        (has_left, dict(col=col - 1)),
        (has_above & has_left, dict(row=row - 1, col=col - 1)),
    )
    barrier = pltpu.get_barrier_semaphore()
    partners = (
        [dict(row=lax.rem(row + k, rows_n)) for k in range(1, rows_n)]
        + [dict(dp=lax.rem(dp + k, dps)) for k in range(1, dps)]
        + [dict(col=lax.rem(col + k, cols_n)) for k in range(1, cols_n)]
    )
    for change in partners:
        pl.semaphore_signal(barrier, inc=1, device_id=peer(**change), device_id_type=MESH)

    @pl.when(senders[2][0])
    def _():
        pl.semaphore_signal(barrier, inc=1, device_id=peer(**senders[2][1]), device_id_type=MESH)

    local[0].wait()
    local[1].wait()
    su_row[...] = up_ref[0, 0].astype(F32)
    sh_row[...] = hid_ref[0, 0].astype(F32)
    for i in range(ur):
        su_col[i : i + 1] = up_ref[0, i].astype(F32)[0:1]
    for i in range(hr):
        sh_col[i : i + 1] = hid_ref[0, i].astype(F32)[0:1]
    su_cor[...] = up_ref[0, 0].astype(F32)[0:8]
    sh_cor[...] = hid_ref[0, 0].astype(F32)[0:8]
    pl.semaphore_wait(barrier, len(partners) + (has_above & has_left).astype(jnp.int32))

    pairs = (
        ((su_row, u_row), (sh_row, h_row)),
        ((su_col, u_col), (sh_col, h_col)),
        ((su_cor, u_cor), (sh_cor, h_cor)),
    )

    def halo_copies(way, change):
        return [
            pltpu.make_async_remote_copy(
                src_ref=src, dst_ref=dst, send_sem=halo_send.at[2 * way + k],
                recv_sem=halo_recv.at[2 * way + k], device_id=peer(**change), device_id_type=MESH,
            )
            for k, (src, dst) in enumerate(pairs[way])
        ]

    for way, (holds, change) in enumerate(targets):
        @pl.when(holds)
        def _():
            for copy in halo_copies(way, change):
                copy.start()

    uext[0:ur, 0:uc] = up_ref[0].astype(F32)
    for h in range(hw // 128):
        aact[h] = jnp.maximum(hid_ref[0, :, :, h * 128 : (h + 1) * 128].astype(F32), 0.0)
    local[2].wait()
    for h in range(pw // 128):
        pix32[h] = pix_ref[0, :, :, h * 128 : (h + 1) * 128].astype(F32)

    for way, (holds, change) in enumerate(senders):
        @pl.when(holds)
        def _():
            for copy in halo_copies(way, change):
                copy.wait_recv()

        @pl.when(jnp.logical_not(holds))
        def _():
            for _, dst in pairs[way]:
                dst[...] = jnp.zeros(dst.shape, dst.dtype)

    uext[ur, 0:uc] = u_row[...]
    for i in range(ur):
        uext[i, uc : uc + 1] = u_col[i : i + 1]
    uext[ur, uc : uc + 1] = u_cor[0:1]
    for (sr, sc), lane in LANE.items():
        part = uext[sr : sr + ur, sc : sc + uc].reshape(ur * uc, uw).astype(BF16)
        ucat[:, lane * uw : (lane + 1) * uw] = part

    if g_ref.shape[0] > 9 * hw:
        g_ref[9 * hw :] = jnp.zeros((g_ref.shape[0] - 9 * hw, width), BF16)

    started = []

    def send(src, dst, send_sem, recv_sem, change):
        copy = pltpu.make_async_remote_copy(
            src_ref=src, dst_ref=dst, send_sem=send_sem, recv_sem=recv_sem,
            device_id=peer(**change), device_id_type=MESH,
        )
        copy.start()
        started.append(copy)
        return copy

    order = [lax.rem(col + j, cols_n) for j in range(1, cols_n)] + [col]

    def window(r, c):
        return pl.ds(pl.multiple_of((r * cols_n + c) * share // 16 * 16, 16), padded)

    sides = (pl.ds(hw, uw), pl.ds(0, hw))
    copies1 = {}

    def send_rows(side):
        for j, c in enumerate(order):
            for k in range(1, rows_n):
                to = lax.rem(row + k, rows_n)
                copies1[side, k, j] = send(
                    g_ref.at[window(to, c), sides[side]], in1.at[k - 1, j, :, sides[side]],
                    s1.at[side, k - 1, j], r1.at[side, k - 1, j], dict(row=to),
                )

    def parity_rows(ref, pr, pc, rows, cols, wide):
        parts = [
            jnp.stack([ref[h, 2 * k + pr, pl.ds(pc, cols, stride=2), :] for k in range(rows)])
            for h in range(wide // 128)
        ]
        return jnp.concatenate(parts, axis=-1).reshape(rows * cols, wide).astype(BF16)

    for pr, pc in PARITIES:
        act = parity_rows(aact, pr, pc, ur, uc, hw)
        terms = terms_of(pr, pc)
        first = terms[0][0]
        total = dot_0(act, ucat[:, first * uw : (first + len(terms)) * uw]) * scale_two
        for n, (_, a, b, _) in enumerate(terms):
            g_ref[pl.ds((3 * a + b) * hw, hw), sides[0]] = total[:, n * uw : (n + 1) * uw].astype(BF16)
    send_rows(0)

    local[3].wait()
    for pr, pc in PARITIES:
        kr = ur + 1 - pr
        total = None
        for _, a, b, (sr, sc) in terms_of(pr, pc):
            u = uext[sr : sr + kr, sc : sc + ucp].reshape(kr * ucp, uw).astype(BF16)
            term = dot_t(u, k2_ref[a, b])
            total = term if total is None else total + term
        total = total.reshape(kr, ucp, hw)
        for k in range(kr):
            for lo in range(0, hw, 128):
                gext[lo // 128, 2 * k + pr, pl.ds(pc, ucp, stride=2), :] = total[k, :, lo : lo + 128]
    for p in range(hr + 1):
        hid = hid_ref[0, p].astype(F32) if p < hr else h_row[...]
        edge = h_col[p : p + 1] if p < hr else h_cor[0:1]
        for lo in range(0, hw, 128):
            cut = slice(lo, lo + 128)
            eext[p, 0:hc, cut] = jnp.where(hid[:, cut] > 0, gext[lo // 128, p, 0:hc], 0.0)
            eext[p, hc : hc + 1, cut] = jnp.where(
                edge[:, cut] > 0, gext[lo // 128, p, hc : hc + 1], 0.0
            )
    for (sr, sc), lane in LANE.items():
        part = eext[sr : sr + hr, sc : sc + hc].reshape(hr * hc, hw).astype(BF16)
        ecat[:, lane * hw : (lane + 1) * hw] = part

    for pr, pc in PARITIES:
        pix = parity_rows(pix32, pr, pc, hr, hc, pw)
        terms = terms_of(pr, pc)
        first = terms[0][0]
        total = dot_0(pix, ecat[:, first * hw : (first + len(terms)) * hw]) * scale_one
        for n, (_, a, b, _) in enumerate(terms):
            g_ref[pl.ds((3 * a + b) * hw, hw), sides[1]] = total[:, n * hw : (n + 1) * hw].astype(BF16)
    send_rows(1)

    def pixel_gradient(pr, pc):
        total = None
        for lane, a, b, _ in terms_of(pr, pc):
            term = dot_t(ecat[:, lane * hw : (lane + 1) * hw], k1_ref[a, b])
            total = term if total is None else total + term
        total = total.reshape(hr, hc, pw)
        for k in range(hr):
            for h in range(pw // 128):
                pix32[h, 2 * k + pr, pl.ds(pc, hc, stride=2), :] = total[k, :, h * 128 : (h + 1) * 128]

    local[4].wait()
    copies2, copies3, copies4 = {}, {}, {}
    for j, c in enumerate(order):
        for pr, pc in PARITIES[j : j + 1]:
            pixel_gradient(pr, pc)
        for k in range(1, rows_n):
            copies1[0, k, j].wait_recv()
            copies1[1, k, j].wait_recv()
        total = g_ref[window(row, c), :].astype(F32)
        for k in range(1, rows_n):
            total = total + in1[k - 1, j].astype(F32)
        for y in range(2):
            for x in range(2):
                acc1[j, y, x] = total[y * half : (y + 1) * half, x * lanes : (x + 1) * lanes].astype(BF16)
        for k in range(1, dps):
            to = lax.rem(dp + k, dps)
            copies2[k, j] = send(
                acc1.at[j, to // 2, to % 2], in2.at[k - 1, j], s2.at[k - 1, j], r2.at[k - 1, j],
                dict(dp=to),
            )
    for pr, pc in PARITIES[cols_n:]:
        pixel_gradient(pr, pc)
    for h in range(pw // 128):
        out_ref[0, :, :, h * 128 : (h + 1) * 128] = pix32[h].astype(BF16)
    out_copy = pltpu.make_async_copy(out_ref, out_hbm, local_sem.at[5])
    out_copy.start()

    for j, c in enumerate(order):
        total = acc1[j, dp // 2, dp % 2].astype(F32)
        for k in range(1, dps):
            copies2[k, j].wait_recv()
            total = total + in2[k - 1, j].astype(F32)
        if j < cols_n - 1:
            acc2[j] = total.astype(BF16)
            copies3[j] = send(acc2.at[j], in3.at[j], s3.at[j], r3.at[j], dict(col=c))
    for j in range(cols_n - 1):
        copies3[j].wait_recv()
        total = total + in3[j].astype(F32)
    mine[...] = total.astype(BF16)
    for k in range(1, dps):
        to = lax.rem(dp + k, dps)
        copies4[k] = send(mine, in4.at[dp // 2, dp % 2], s4.at[k - 1], r4.at[k - 1], dict(dp=to))
    in4[dp // 2, dp % 2] = mine[...]
    for k in range(1, dps):
        copies4[k].wait_recv()
    for y in range(2):
        whole = jnp.concatenate([in4[y, 0], in4[y, 1]], axis=-1).astype(F32)
        g1_out[y * half : (y + 1) * half] = whole[:, 0:hw]
        g2_out[y * half : (y + 1) * half] = whole[:, hw:]
    out_copy.wait()
    for copy in started:
        copy.wait_send()
    for way, (holds, change) in enumerate(targets):
        @pl.when(holds)
        def _():
            for copy in halo_copies(way, change):
                copy.wait_send()


def fused(pixels, hidden, upstream, kernel_first, kernel_second, mesh):
    dps, rows_n, cols_n = (mesh.shape[name] for name in NAMES)
    _, ur, uc, uw = upstream.shape
    _, hr, hc, hw = hidden.shape
    _, pr, pc, pw = pixels.shape
    scale_one = 1.0 / math.sqrt(mesh.size * hr * hc)
    scale_two = 1.0 / math.sqrt(mesh.size * ur * uc)
    ucp = (uc // 8 + 1) * 8
    share = 9 * hw // (rows_n * cols_n)
    exact = share % 32 == 0
    padded = share if exact else -(-(share + 15) // 32) * 32
    g_rows = 9 * hw + (0 if exact else padded)
    width = hw + uw
    half, lanes = padded // 2, width // 2
    halo = [(uc, uw), (ur, uw), (8, uw), (hc, hw), (hr, hw), (8, hw)]
    dma = pltpu.SemaphoreType.DMA
    anywhere = pl.BlockSpec(memory_space=pl.ANY)
    vmem = pl.BlockSpec(memory_space=pltpu.VMEM)
    grad_pixels, g1, g2 = pl.pallas_call(
        functools.partial(
            fused_kernel, dps, rows_n, cols_n, share, padded, scale_one, scale_two
        ),
        out_shape=[
            jax.ShapeDtypeStruct(pixels.shape, BF16),
            jax.ShapeDtypeStruct((padded, hw), F32),
            jax.ShapeDtypeStruct((padded, uw), F32),
        ],
        in_specs=[anywhere] * 5,
        out_specs=[anywhere, vmem, vmem],
        scratch_shapes=[
            pltpu.VMEM(a.shape, BF16)
            for a in (pixels, hidden, upstream, kernel_first, kernel_second, pixels)
        ]
        + [pltpu.VMEM(s, F32) for s in halo + halo]
        + [
            pltpu.VMEM((ur + 2, ucp + 8, uw), F32),
            pltpu.VMEM((hw // 128, hr + 2, 2 * ucp, 128), F32),
            pltpu.VMEM((hr + 1, hc + 8, hw), F32),
            pltpu.VMEM((ur * uc, 4 * uw), BF16),
            pltpu.VMEM((hr * hc, 4 * hw), BF16),
            pltpu.VMEM((hw // 128, hr, hc, 128), F32),
            pltpu.VMEM((pw // 128, pr, pc, 128), F32),
            pltpu.VMEM((g_rows, width), BF16),
            pltpu.VMEM((cols_n, 2, 2, half, lanes), BF16),
            pltpu.VMEM((rows_n - 1, cols_n, padded, width), BF16),
            pltpu.VMEM((cols_n - 1, half, lanes), BF16),
            pltpu.VMEM((dps - 1, cols_n, half, lanes), BF16),
            pltpu.VMEM((cols_n - 1, half, lanes), BF16),
            pltpu.VMEM((half, lanes), BF16),
            pltpu.VMEM((2, 2, half, lanes), BF16),
            dma((6,)), dma((6,)), dma((6,)),
            dma((2, rows_n - 1, cols_n)), dma((2, rows_n - 1, cols_n)),
            dma((dps - 1, cols_n)), dma((dps - 1, cols_n)),
            dma((cols_n - 1,)), dma((cols_n - 1,)),
            dma((dps - 1,)), dma((dps - 1,)),
        ],
        compiler_params=pltpu.CompilerParams(
            collective_id=0, has_side_effects=True, vmem_limit_bytes=56 * 2**20
        ),
    )(pixels, hidden, upstream, kernel_first, kernel_second)
    if not exact:
        at = (lax.axis_index("row") * cols_n + lax.axis_index("col")) * share % 16
        g1, g2 = (lax.dynamic_slice_in_dim(g, at, share, 0) for g in (g1, g2))
    return grad_pixels, g1, g2


def solution(mesh):
    def per_device(*args):
        return tuple(fused(*args, mesh))

    in_specs = (P("dp", "row", "col", None),) * 3 + (P(), P())
    out_specs = (P("dp", "row", "col", None), P(("row", "col"), None), P(("row", "col"), None))
    return jax.shard_map(
        per_device, mesh=mesh, in_specs=in_specs, out_specs=out_specs, check_vma=False
    )
```

```python
import functools
import math

import jax
import jax.numpy as jnp
from jax import lax
from jax.experimental import pallas as pl
from jax.experimental.pallas import tpu as pltpu
from jax.sharding import PartitionSpec as P

MESH = pl.DeviceIdType.MESH
F32 = jnp.float32
BF16 = jnp.bfloat16
NAMES = ("dp", "row", "col")


def peer(**changes):
    return tuple(changes.get(name, lax.axis_index(name)) for name in NAMES)


TAPS = {0: ((1, 0),), 1: ((2, 0), (0, 1))}
LANE = {(0, 1): 0, (0, 0): 1, (1, 0): 2, (1, 1): 3}


def terms_of(pr, pc):
    found = []
    for a, sr in TAPS[pr]:
        for b, sc in TAPS[pc]:
            found.append((LANE[(sr, sc)], a, b, (sr, sc)))
    return sorted(found)


PARITIES = ((0, 0), (0, 1), (1, 0), (1, 1))


def dot_t(x, w):
    return lax.dot_general(x, w, (((1,), (1,)), ((), ())), preferred_element_type=F32)


def dot_0(x, y):
    return lax.dot_general(x, y, (((0,), (0,)), ((), ())), preferred_element_type=F32)


def fused_kernel(
    dps, rows_n, cols_n, share, padded, scale_one, scale_two,
    pix_hbm, hid_hbm, up_hbm, k1_hbm, k2_hbm, out_hbm, g1_out, g2_out,
    pix_ref, hid_ref, up_ref, k1_ref, k2_ref, out_ref,
    u_row, u_col, u_cor, h_row, h_col, h_cor,
    su_row, su_col, su_cor, sh_row, sh_col, sh_cor,
    uext, gext, eext, ucat, ecat, aact, pix32, g_ref,
    acc1, in1, acc2, in2, in3, mine, in4,
    local_sem, halo_send, halo_recv, s1, r1, s2, r2, s3, r3, s4, r4,
):
    dp, row, col = (lax.axis_index(name) for name in NAMES)
    _, ur, uc, uw = up_ref.shape
    _, hr, hc, hw = hid_ref.shape
    pw = pix_ref.shape[-1]
    ucp = uext.shape[1] - 8
    width = hw + uw
    half, lanes = padded // 2, width // 2
    local = [
        pltpu.make_async_copy(src, dst, local_sem.at[n])
        for n, (src, dst) in enumerate(
            ((up_hbm, up_ref), (hid_hbm, hid_ref), (pix_hbm, pix_ref), (k2_hbm, k2_ref), (k1_hbm, k1_ref))
        )
    ]
    for copy in local:
        copy.start()

    has_above, has_left = row > 0, col > 0
    has_below, has_right = row < rows_n - 1, col < cols_n - 1
    senders = (
        (has_below, dict(row=row + 1)),
        (has_right, dict(col=col + 1)),
        (has_below & has_right, dict(row=row + 1, col=col + 1)),
    )
    targets = (
        (has_above, dict(row=row - 1)),
        (has_left, dict(col=col - 1)),
        (has_above & has_left, dict(row=row - 1, col=col - 1)),
    )
    barrier = pltpu.get_barrier_semaphore()
    partners = (
        [dict(row=lax.rem(row + k, rows_n)) for k in range(1, rows_n)]
        + [dict(dp=lax.rem(dp + k, dps)) for k in range(1, dps)]
        + [dict(col=lax.rem(col + k, cols_n)) for k in range(1, cols_n)]
    )
    for change in partners:
        pl.semaphore_signal(barrier, inc=1, device_id=peer(**change), device_id_type=MESH)

    @pl.when(senders[2][0])
    def _():
        pl.semaphore_signal(barrier, inc=1, device_id=peer(**senders[2][1]), device_id_type=MESH)

    local[0].wait()
    local[1].wait()
    su_row[...] = up_ref[0, 0].astype(F32)
    sh_row[...] = hid_ref[0, 0].astype(F32)
    for i in range(ur):
        su_col[i : i + 1] = up_ref[0, i].astype(F32)[0:1]
    for i in range(hr):
        sh_col[i : i + 1] = hid_ref[0, i].astype(F32)[0:1]
    su_cor[...] = up_ref[0, 0].astype(F32)[0:8]
    sh_cor[...] = hid_ref[0, 0].astype(F32)[0:8]
    pl.semaphore_wait(barrier, len(partners) + (has_above & has_left).astype(jnp.int32))

    pairs = (
        ((su_row, u_row), (sh_row, h_row)),
        ((su_col, u_col), (sh_col, h_col)),
        ((su_cor, u_cor), (sh_cor, h_cor)),
    )

    def halo_copies(way, change):
        return [
            pltpu.make_async_remote_copy(
                src_ref=src, dst_ref=dst, send_sem=halo_send.at[2 * way + k],
                recv_sem=halo_recv.at[2 * way + k], device_id=peer(**change), device_id_type=MESH,
            )
            for k, (src, dst) in enumerate(pairs[way])
        ]

    for way, (holds, change) in enumerate(targets):
        @pl.when(holds)
        def _():
            for copy in halo_copies(way, change):
                copy.start()

    uext[0:ur, 0:uc] = up_ref[0].astype(F32)
    for h in range(hw // 128):
        aact[h] = jnp.maximum(hid_ref[0, :, :, h * 128 : (h + 1) * 128].astype(F32), 0.0)
    local[2].wait()
    for h in range(pw // 128):
        pix32[h] = pix_ref[0, :, :, h * 128 : (h + 1) * 128].astype(F32)

    for way, (holds, change) in enumerate(senders):
        @pl.when(holds)
        def _():
            for copy in halo_copies(way, change):
                copy.wait_recv()

        @pl.when(jnp.logical_not(holds))
        def _():
            for _, dst in pairs[way]:
                dst[...] = jnp.zeros(dst.shape, dst.dtype)

    uext[ur, 0:uc] = u_row[...]
    for i in range(ur):
        uext[i, uc : uc + 1] = u_col[i : i + 1]
    uext[ur, uc : uc + 1] = u_cor[0:1]
    for (sr, sc), lane in LANE.items():
        part = uext[sr : sr + ur, sc : sc + uc].reshape(ur * uc, uw).astype(BF16)
        ucat[:, lane * uw : (lane + 1) * uw] = part

    if g_ref.shape[0] > 9 * hw:
        g_ref[9 * hw :] = jnp.zeros((g_ref.shape[0] - 9 * hw, width), BF16)

    started = []

    def send(src, dst, send_sem, recv_sem, change):
        copy = pltpu.make_async_remote_copy(
            src_ref=src, dst_ref=dst, send_sem=send_sem, recv_sem=recv_sem,
            device_id=peer(**change), device_id_type=MESH,
        )
        copy.start()
        started.append(copy)
        return copy

    order = [lax.rem(col + j, cols_n) for j in range(1, cols_n)] + [col]

    def window(r, c):
        return pl.ds(pl.multiple_of((r * cols_n + c) * share // 16 * 16, 16), padded)

    sides = (pl.ds(hw, uw), pl.ds(0, hw))
    copies1 = {}

    def send_rows(side):
        for j, c in enumerate(order):
            for k in range(1, rows_n):
                to = lax.rem(row + k, rows_n)
                copies1[side, k, j] = send(
                    g_ref.at[window(to, c), sides[side]], in1.at[k - 1, j, :, sides[side]],
                    s1.at[side, k - 1, j], r1.at[side, k - 1, j], dict(row=to),
                )

    def parity_rows(ref, pr, pc, rows, cols, wide):
        parts = [
            jnp.stack([ref[h, 2 * k + pr, pl.ds(pc, cols, stride=2), :] for k in range(rows)])
            for h in range(wide // 128)
        ]
        return jnp.concatenate(parts, axis=-1).reshape(rows * cols, wide).astype(BF16)

    for pr, pc in PARITIES:
        act = parity_rows(aact, pr, pc, ur, uc, hw)
        terms = terms_of(pr, pc)
        first = terms[0][0]
        total = dot_0(act, ucat[:, first * uw : (first + len(terms)) * uw]) * scale_two
        for n, (_, a, b, _) in enumerate(terms):
            g_ref[pl.ds((3 * a + b) * hw, hw), sides[0]] = total[:, n * uw : (n + 1) * uw].astype(BF16)
    send_rows(0)

    local[3].wait()
    for pr, pc in PARITIES:
        kr = ur + 1 - pr
        total = None
        for _, a, b, (sr, sc) in terms_of(pr, pc):
            u = uext[sr : sr + kr, sc : sc + ucp].reshape(kr * ucp, uw).astype(BF16)
            term = dot_t(u, k2_ref[a, b])
            total = term if total is None else total + term
        total = total.reshape(kr, ucp, hw)
        for k in range(kr):
            for lo in range(0, hw, 128):
                gext[lo // 128, 2 * k + pr, pl.ds(pc, ucp, stride=2), :] = total[k, :, lo : lo + 128]
    for p in range(hr + 1):
        hid = hid_ref[0, p].astype(F32) if p < hr else h_row[...]
        edge = h_col[p : p + 1] if p < hr else h_cor[0:1]
        for lo in range(0, hw, 128):
            cut = slice(lo, lo + 128)
            eext[p, 0:hc, cut] = jnp.where(hid[:, cut] > 0, gext[lo // 128, p, 0:hc], 0.0)
            eext[p, hc : hc + 1, cut] = jnp.where(
                edge[:, cut] > 0, gext[lo // 128, p, hc : hc + 1], 0.0
            )
    for (sr, sc), lane in LANE.items():
        part = eext[sr : sr + hr, sc : sc + hc].reshape(hr * hc, hw).astype(BF16)
        ecat[:, lane * hw : (lane + 1) * hw] = part

    parts = (pl.ds(0, uw // 2), pl.ds(uw // 2, hw // 2))
    copies2 = {}

    def row_sums(side, j):
        total = g_ref[window(row, order[j]), sides[side]].astype(F32)
        for k in range(1, rows_n):
            copies1[side, k, j].wait_recv()
            total = total + in1[k - 1, j, :, sides[side]].astype(F32)
        wide = total.shape[-1] // 2
        for y in range(2):
            for x in range(2):
                acc1[j, y, x, :, parts[side]] = total[
                    y * half : (y + 1) * half, x * wide : (x + 1) * wide
                ].astype(BF16)
        for k in range(1, dps):
            to = lax.rem(dp + k, dps)
            copies2[side, k, j] = send(
                acc1.at[j, to // 2, to % 2, :, parts[side]], in2.at[k - 1, j, :, parts[side]],
                s2.at[side, k - 1, j], r2.at[side, k - 1, j], dict(dp=to),
            )

    for j in range(cols_n):
        row_sums(0, j)

    for pr, pc in PARITIES:
        pix = parity_rows(pix32, pr, pc, hr, hc, pw)
        terms = terms_of(pr, pc)
        first = terms[0][0]
        total = dot_0(pix, ecat[:, first * hw : (first + len(terms)) * hw]) * scale_one
        for n, (_, a, b, _) in enumerate(terms):
            g_ref[pl.ds((3 * a + b) * hw, hw), sides[1]] = total[:, n * hw : (n + 1) * hw].astype(BF16)
    send_rows(1)

    def pixel_gradient(pr, pc):
        total = None
        for lane, a, b, _ in terms_of(pr, pc):
            term = dot_t(ecat[:, lane * hw : (lane + 1) * hw], k1_ref[a, b])
            total = term if total is None else total + term
        total = total.reshape(hr, hc, pw)
        for k in range(hr):
            for h in range(pw // 128):
                pix32[h, 2 * k + pr, pl.ds(pc, hc, stride=2), :] = total[k, :, h * 128 : (h + 1) * 128]

    local[4].wait()
    copies3, copies4 = {}, {}
    for j, c in enumerate(order):
        for pr, pc in PARITIES[j : j + 1]:
            pixel_gradient(pr, pc)
        row_sums(1, j)
    for pr, pc in PARITIES[cols_n:]:
        pixel_gradient(pr, pc)
    for h in range(pw // 128):
        out_ref[0, :, :, h * 128 : (h + 1) * 128] = pix32[h].astype(BF16)
    out_copy = pltpu.make_async_copy(out_ref, out_hbm, local_sem.at[5])
    out_copy.start()

    for j, c in enumerate(order):
        total = acc1[j, dp // 2, dp % 2].astype(F32)
        for k in range(1, dps):
            copies2[0, k, j].wait_recv()
            copies2[1, k, j].wait_recv()
            total = total + in2[k - 1, j].astype(F32)
        if j < cols_n - 1:
            acc2[j] = total.astype(BF16)
            copies3[j] = send(acc2.at[j], in3.at[j], s3.at[j], r3.at[j], dict(col=c))
    for j in range(cols_n - 1):
        copies3[j].wait_recv()
        total = total + in3[j].astype(F32)
    mine[...] = total.astype(BF16)
    for k in range(1, dps):
        to = lax.rem(dp + k, dps)
        copies4[k] = send(mine, in4.at[dp // 2, dp % 2], s4.at[k - 1], r4.at[k - 1], dict(dp=to))
    in4[dp // 2, dp % 2] = mine[...]
    for k in range(1, dps):
        copies4[k].wait_recv()
    for y in range(2):
        for side, out in enumerate((g2_out, g1_out)):
            both = [in4[y, x, :, parts[side]] for x in range(2)]
            out[y * half : (y + 1) * half] = jnp.concatenate(both, axis=-1).astype(F32)
    out_copy.wait()
    for copy in started:
        copy.wait_send()
    for way, (holds, change) in enumerate(targets):
        @pl.when(holds)
        def _():
            for copy in halo_copies(way, change):
                copy.wait_send()


def fused(pixels, hidden, upstream, kernel_first, kernel_second, mesh):
    dps, rows_n, cols_n = (mesh.shape[name] for name in NAMES)
    _, ur, uc, uw = upstream.shape
    _, hr, hc, hw = hidden.shape
    _, pr, pc, pw = pixels.shape
    scale_one = 1.0 / math.sqrt(mesh.size * hr * hc)
    scale_two = 1.0 / math.sqrt(mesh.size * ur * uc)
    ucp = (uc // 8 + 1) * 8
    share = 9 * hw // (rows_n * cols_n)
    exact = share % 32 == 0
    padded = share if exact else -(-(share + 15) // 32) * 32
    g_rows = 9 * hw + (0 if exact else padded)
    width = hw + uw
    half, lanes = padded // 2, width // 2
    halo = [(uc, uw), (ur, uw), (8, uw), (hc, hw), (hr, hw), (8, hw)]
    dma = pltpu.SemaphoreType.DMA
    anywhere = pl.BlockSpec(memory_space=pl.ANY)
    vmem = pl.BlockSpec(memory_space=pltpu.VMEM)
    grad_pixels, g1, g2 = pl.pallas_call(
        functools.partial(
            fused_kernel, dps, rows_n, cols_n, share, padded, scale_one, scale_two
        ),
        out_shape=[
            jax.ShapeDtypeStruct(pixels.shape, BF16),
            jax.ShapeDtypeStruct((padded, hw), F32),
            jax.ShapeDtypeStruct((padded, uw), F32),
        ],
        in_specs=[anywhere] * 5,
        out_specs=[anywhere, vmem, vmem],
        scratch_shapes=[
            pltpu.VMEM(a.shape, BF16)
            for a in (pixels, hidden, upstream, kernel_first, kernel_second, pixels)
        ]
        + [pltpu.VMEM(s, F32) for s in halo + halo]
        + [
            pltpu.VMEM((ur + 2, ucp + 8, uw), F32),
            pltpu.VMEM((hw // 128, hr + 2, 2 * ucp, 128), F32),
            pltpu.VMEM((hr + 1, hc + 8, hw), F32),
            pltpu.VMEM((ur * uc, 4 * uw), BF16),
            pltpu.VMEM((hr * hc, 4 * hw), BF16),
            pltpu.VMEM((hw // 128, hr, hc, 128), F32),
            pltpu.VMEM((pw // 128, pr, pc, 128), F32),
            pltpu.VMEM((g_rows, width), BF16),
            pltpu.VMEM((cols_n, 2, 2, half, lanes), BF16),
            pltpu.VMEM((rows_n - 1, cols_n, padded, width), BF16),
            pltpu.VMEM((cols_n - 1, half, lanes), BF16),
            pltpu.VMEM((dps - 1, cols_n, half, lanes), BF16),
            pltpu.VMEM((cols_n - 1, half, lanes), BF16),
            pltpu.VMEM((half, lanes), BF16),
            pltpu.VMEM((2, 2, half, lanes), BF16),
            dma((6,)), dma((6,)), dma((6,)),
            dma((2, rows_n - 1, cols_n)), dma((2, rows_n - 1, cols_n)),
            dma((2, dps - 1, cols_n)), dma((2, dps - 1, cols_n)),
            dma((cols_n - 1,)), dma((cols_n - 1,)),
            dma((dps - 1,)), dma((dps - 1,)),
        ],
        compiler_params=pltpu.CompilerParams(
            collective_id=0, has_side_effects=True, vmem_limit_bytes=56 * 2**20
        ),
    )(pixels, hidden, upstream, kernel_first, kernel_second)
    if not exact:
        at = (lax.axis_index("row") * cols_n + lax.axis_index("col")) * share % 16
        g1, g2 = (lax.dynamic_slice_in_dim(g, at, share, 0) for g in (g1, g2))
    return grad_pixels, g1, g2


def solution(mesh):
    def per_device(*args):
        return tuple(fused(*args, mesh))

    in_specs = (P("dp", "row", "col", None),) * 3 + (P(), P())
    out_specs = (P("dp", "row", "col", None), P(("row", "col"), None), P(("row", "col"), None))
    return jax.shard_map(
        per_device, mesh=mesh, in_specs=in_specs, out_specs=out_specs, check_vma=False
    )
```
